32 devices in a mesh: row: 8 (over y, x, core), col: 4 (over z).
Axes of the slice: x: 2, y: 2, z: 4, core: 2. Of those that a mesh axis runs over, the one named last changes fastest.
Arguments:
- inputs: bfloat16 [1024, 4096], P('row', 'col'), may hold values from -6 to 6
- grad_output: bfloat16 [1024, 4096], P('row', 'col'), may hold values from -6 to 6
- gate_pre: bfloat16 [1024, 14336], P('col', 'row'), may hold values from -6 to 6
- up_pre: bfloat16 [1024, 14336], P('col', 'row'), may hold values from -6 to 6
- gate_weight: bfloat16 [14336, 4096], P('row', 'col'), may hold values from -0.09375 to 0.09375
- up_weight: bfloat16 [14336, 4096], P('row', 'col'), may hold values from -0.09375 to 0.09375
- down_weight: bfloat16 [14336, 4096], P('row', 'col'), may hold values from -0.046875 to 0.046875
Outputs:
- grad_input: float32 [1024, 4096], P('row', 'col')
- grad_gate_weight: float32 [14336, 4096], P('row', 'col')
- grad_up_weight: float32 [14336, 4096], P('row', 'col')
- grad_down_weight: float32 [14336, 4096], P('row', 'col')
The draws below stay inside these ranges and needn't reach their ends.
All inputs are finite; a program needn't handle non-finite values.
Results may differ from the reference program's by a relative error of at most 0.0029.
Values may be sent and summed in bfloat16 or wider, within the bound.
A program may use at most 128 MiB of HBM per device.

```python
import math
import jax
import jax.numpy as jnp

D = 4096
FF = 14336
TOKENS = 1024


def with_spikes(values, stream_key, source, target, parts, factor):
    def block_of(dim):
        return (jnp.arange(values.shape[dim]) // (values.shape[dim] // parts)).reshape((-1,) + (1,) * (values.ndim - 1 - dim))

    one_side = jax.random.permutation(stream_key, parts)[block_of(target)]
    second = (block_of(target) + parts // 2) % parts
    return jnp.where((block_of(source) == one_side) | (block_of(source) == second), factor * values, values)


def shard_levels(own_key, shape, shards, smallest, largest):
    loudness = 1.0
    for dim, shards_of in shards:
        draws = jax.random.uniform(jax.random.fold_in(jax.random.fold_in(own_key, 6), dim), (shards_of,), jnp.float32, smallest / len(shards), largest / len(shards))
        loudness = loudness * jnp.repeat(jnp.exp(draws), shape[dim] // shards_of).reshape((-1,) + (1,) * (len(shape) - 1 - dim))
    return loudness


def bell_draw(own_key, extent, width, limit, cuts=(), dtype=jnp.bfloat16):
    entries = width * jax.random.normal(own_key, extent, jnp.float32)
    if cuts:
        entries = entries * shard_levels(own_key, extent, cuts, -0.22, 0.18)
    return jnp.clip(entries, -limit, limit).astype(dtype)


def noise_with(rng, shape, spread, limit, split, heavy, held_as=jnp.bfloat16):
    drawn = spread * jax.random.normal(rng, shape, jnp.float32)
    if split:
        drawn = drawn * shard_levels(rng, shape, split, -0.22, 0.18)
    return jnp.clip(with_spikes(drawn, jax.random.fold_in(rng, 3), *heavy), -limit, limit).astype(held_as)


def setup_inputs(seed: int = 0) -> dict:
    key_list = jax.random.split(jax.random.key(seed), 8)
    return {
        "inputs": bell_draw(key_list[0], (TOKENS, D), 1.0, 6.0, ((0, 8), (1, 4))),
        "grad_output": noise_with(key_list[1], (TOKENS, D), 1.0, 6.0, ((0, 8), (1, 4)), (1, 0, 8, 2.0)),
        "gate_pre": bell_draw(key_list[2], (TOKENS, FF), 1.0, 6.0, ((0, 4), (1, 8))),
        "up_pre": noise_with(key_list[3], (TOKENS, FF), 1.0, 6.0, ((0, 4), (1, 8)), (1, 0, 8, 2.0)),
        "gate_weight": bell_draw(key_list[4], (FF, D), D ** -0.5, 0.09375, ((0, 8), (1, 4))),
        "up_weight": bell_draw(key_list[5], (FF, D), D ** -0.5, 0.09375, ((0, 8), (1, 4))),
        "down_weight": bell_draw(key_list[6], (FF, D), FF ** -0.5, 0.046875, ((0, 8), (1, 4))),
    }


def reference(inputs, grad_output, gate_pre, up_pre, gate_weight, up_weight, down_weight):
    gate_value = gate_pre.astype(jnp.float32)
    up_value = up_pre.astype(jnp.float32)
    sigmoid_gate = jax.nn.sigmoid(gate_value)
    silu_gate = gate_value * sigmoid_gate
    hidden = (silu_gate * up_value).astype(jnp.bfloat16)
    grad_hidden = jnp.dot(grad_output, down_weight.T, preferred_element_type=jnp.float32)
    grad_gate_pre = (grad_hidden * up_value * sigmoid_gate * (1.0 + gate_value * (1.0 - sigmoid_gate))).astype(jnp.bfloat16)
    grad_up_pre = (grad_hidden * silu_gate).astype(jnp.bfloat16)
    grad_input = jnp.dot(grad_gate_pre, gate_weight, preferred_element_type=jnp.float32) + jnp.dot(grad_up_pre, up_weight, preferred_element_type=jnp.float32)
    factor = 1.0 / math.sqrt(TOKENS)
    grad_gate_weight = jnp.dot(grad_gate_pre.T, inputs, preferred_element_type=jnp.float32) * factor
    grad_up_weight = jnp.dot(grad_up_pre.T, inputs, preferred_element_type=jnp.float32) * factor
    grad_down_weight = jnp.dot(hidden.T, grad_output, preferred_element_type=jnp.float32) * factor
    return (grad_input, grad_gate_weight, grad_up_weight, grad_down_weight)
```

```python
import math

import jax
import jax.numpy as jnp
from jax import lax
from jax.sharding import PartitionSpec as P


def outer_sum(left_rows, right_rows):
    return lax.dot_general(
        left_rows, right_rows, (((0,), (0,)), ((), ())), preferred_element_type=jnp.float32
    )


def inner_last(left_rows, right_rows):
    return lax.dot_general(
        left_rows, right_rows, (((1,), (1,)), ((), ())), preferred_element_type=jnp.float32
    )


def line_gather(own, n, me):
    from_left, from_right = [own], [own]
    for step in range(1, n):
        from_left.append(
            lax.ppermute(from_left[-1], "col", [(i, i + 1) for i in range(step - 1, n - 1)])
        )
        from_right.append(
            lax.ppermute(from_right[-1], "col", [(i, i - 1) for i in range(1, n - step + 1)])
        )
    return [own] + [
        jnp.where(me + k < n, from_right[k], from_left[n - k]) for k in range(1, n)
    ]


def line_scatter_sum(whole, n, me):
    rows = whole.shape[0] // n

    def block(target):
        return lax.dynamic_slice_in_dim(whole, jnp.clip(target, 0, n - 1) * rows, rows, axis=0)

    right = left = None
    for step in range(1, n):
        to_right, to_left = block(me + n - step), block(me - n + step)
        if step > 1:
            to_right, to_left = to_right + right, to_left + left
        right = lax.ppermute(to_right, "col", [(i, i + 1) for i in range(step)])
        left = lax.ppermute(to_left, "col", [(i, i - 1) for i in range(n - step, n)])
    own = block(me)
    return own if n == 1 else own + right + left


def cuts(width, parts):
    unit = 256 if width % 256 == 0 else 128 if width % 128 == 0 else 1
    units = width // unit
    parts = min(parts, units)
    edges = [unit * (units * p // parts) for p in range(parts + 1)]
    return list(zip(edges[:-1], edges[1:]))


def shards(inputs, grad_output, gate_pre, up_pre, gate_weight, up_weight, down_weight):
    n = lax.axis_size("col")
    me = lax.axis_index("col")
    output_cols = lax.all_gather(grad_output, "row", axis=0, tiled=True)
    input_cols = lax.all_gather(inputs, "row", axis=0, tiled=True)
    tokens = input_cols.shape[0]
    block_rows = tokens // n

    gate_value = gate_pre.astype(jnp.float32)
    up_value = up_pre.astype(jnp.float32)
    sigmoid_gate = jax.nn.sigmoid(gate_value)
    hidden = (gate_value * sigmoid_gate * up_value).astype(jnp.bfloat16)
    hidden_rows = jnp.concatenate(line_gather(hidden, n, me), axis=0)

    pieces = []
    partial_input = None
    for lo, hi in cuts(gate_pre.shape[1], 3):
        grad_hidden = line_scatter_sum(inner_last(output_cols, down_weight[lo:hi]), n, me)
        g = gate_pre[:, lo:hi].astype(jnp.float32)
        u = up_pre[:, lo:hi].astype(jnp.float32)
        s = jax.nn.sigmoid(g)
        grad_gate_pre = (grad_hidden * u * s * (1.0 + g * (1.0 - s))).astype(jnp.bfloat16)
        grad_up_pre = (grad_hidden * (g * s)).astype(jnp.bfloat16)
        both = jnp.concatenate([grad_gate_pre, grad_up_pre], axis=1)
        piece = jnp.concatenate(line_gather(both, n, me), axis=0)
        gate_piece, up_piece = piece[:, : hi - lo], piece[:, hi - lo :]
        part = jnp.dot(
            gate_piece, gate_weight[lo:hi], preferred_element_type=jnp.float32
        ) + jnp.dot(up_piece, up_weight[lo:hi], preferred_element_type=jnp.float32)
        partial_input = part if partial_input is None else partial_input + part
        pieces.append((gate_piece, up_piece))

    shift = me * block_rows
    partial_input = lax.dynamic_slice_in_dim(
        jnp.concatenate([partial_input, partial_input], axis=0), tokens - shift, tokens, axis=0
    )
    grad_input = lax.psum_scatter(partial_input, "row", scatter_dimension=0, tiled=True)

    def turned(rows):
        return lax.dynamic_slice_in_dim(
            jnp.concatenate([rows, rows], axis=0), shift, tokens, axis=0
        )

    input_rows, output_rows = turned(input_cols), turned(output_cols)
    gate_rows = jnp.concatenate([p[0] for p in pieces], axis=1)
    up_rows = jnp.concatenate([p[1] for p in pieces], axis=1)
    factor = 1.0 / math.sqrt(tokens)
    return (
        grad_input,
        outer_sum(gate_rows, input_rows) * factor,
        outer_sum(up_rows, input_rows) * factor,
        outer_sum(hidden_rows, output_rows) * factor,
    )


def solution(mesh):
    split, turned = P("row", "col"), P("col", "row")
    return jax.shard_map(
        shards,
        mesh=mesh,
        in_specs=(split, split, turned, turned, split, split, split),
        out_specs=(split, split, split, split),
        check_vma=False,
    )
```

```python
import math

import jax
import jax.numpy as jnp
from jax import lax
from jax.sharding import PartitionSpec as P


def outer_sum(left_rows, right_rows):
    return lax.dot_general(
        left_rows, right_rows, (((0,), (0,)), ((), ())), preferred_element_type=jnp.float32
    )


def inner_last(left_rows, right_rows):
    return lax.dot_general(
        left_rows, right_rows, (((1,), (1,)), ((), ())), preferred_element_type=jnp.float32
    )


def line_steps(own, n):
    from_left, from_right = [own], [own]
    for step in range(1, n):
        from_left.append(
            lax.ppermute(from_left[-1], "col", [(i, i + 1) for i in range(step - 1, n - 1)])
        )
        from_right.append(
            lax.ppermute(from_right[-1], "col", [(i, i - 1) for i in range(1, n - step + 1)])
        )
    return from_left, from_right


def in_turn(steps, n, me):
    from_left, from_right = steps
    return jnp.concatenate(
        [from_left[0]]
        + [jnp.where(me + k < n, from_right[k], from_left[n - k]) for k in range(1, n)],
        axis=0,
    )


def cuts(width, parts):
    unit = 256 if width % 256 == 0 else 128 if width % 128 == 0 else 1
    units = width // unit
    parts = min(parts, units)
    edges = [unit * -(-units * p // parts) for p in range(parts + 1)]
    return list(zip(edges[:-1], edges[1:]))


def shards(inputs, grad_output, gate_pre, up_pre, gate_weight, up_weight, down_weight):
    n = lax.axis_size("col")
    me = lax.axis_index("col")
    output_cols = lax.all_gather(grad_output, "row", axis=0, tiled=True)
    tokens = output_cols.shape[0]
    block_rows = tokens // n

    gate_value = gate_pre.astype(jnp.float32)
    up_value = up_pre.astype(jnp.float32)
    sigmoid_gate = jax.nn.sigmoid(gate_value)
    hidden = (gate_value * sigmoid_gate * up_value).astype(jnp.bfloat16)
    hidden_steps = line_steps(hidden, n)

    chunks = cuts(gate_pre.shape[1], 2)
    sums = [
        lax.psum_scatter(
            inner_last(output_cols, down_weight[lo:hi]), "col", scatter_dimension=0, tiled=True
        )
        for lo, hi in chunks
    ]
    sums[-1], inputs = lax.optimization_barrier((sums[-1], inputs))
    input_cols = lax.all_gather(inputs, "row", axis=0, tiled=True)
    hidden_rows = in_turn(hidden_steps, n, me)

    pieces = []
    partial_input = None
    earlier = hidden_steps
    for (lo, hi), grad_hidden in zip(chunks, sums):
        behind = sum(0.0 * side[-1][:1, :1].astype(jnp.float32) for side in earlier)
        grad_hidden = grad_hidden + behind
        g = gate_pre[:, lo:hi].astype(jnp.float32)
        u = up_pre[:, lo:hi].astype(jnp.float32)
        s = jax.nn.sigmoid(g)
        grad_gate_pre = (grad_hidden * u * s * (1.0 + g * (1.0 - s))).astype(jnp.bfloat16)
        grad_up_pre = (grad_hidden * (g * s)).astype(jnp.bfloat16)
        both = jnp.concatenate([grad_gate_pre, grad_up_pre], axis=1)
        earlier = line_steps(both, n)
        piece = in_turn(earlier, n, me)
        gate_piece, up_piece = piece[:, : hi - lo], piece[:, hi - lo :]
        part = jnp.dot(
            gate_piece, gate_weight[lo:hi], preferred_element_type=jnp.float32
        ) + jnp.dot(up_piece, up_weight[lo:hi], preferred_element_type=jnp.float32)
        partial_input = part if partial_input is None else partial_input + part
        pieces.append((gate_piece, up_piece))

    shift = me * block_rows
    partial_input = lax.dynamic_slice_in_dim(
        jnp.concatenate([partial_input, partial_input], axis=0), tokens - shift, tokens, axis=0
    )
    grad_input = lax.psum_scatter(partial_input, "row", scatter_dimension=0, tiled=True)

    def turned(rows):
        return lax.dynamic_slice_in_dim(
            jnp.concatenate([rows, rows], axis=0), shift, tokens, axis=0
        )

    input_rows, output_rows = turned(input_cols), turned(output_cols)
    gate_rows = jnp.concatenate([p[0] for p in pieces], axis=1)
    up_rows = jnp.concatenate([p[1] for p in pieces], axis=1)
    factor = 1.0 / math.sqrt(tokens)
    return (
        grad_input,
        outer_sum(gate_rows, input_rows) * factor,
        outer_sum(up_rows, input_rows) * factor,
        outer_sum(hidden_rows, output_rows) * factor,
    )


def solution(mesh):
    split, turned = P("row", "col"), P("col", "row")
    return jax.shard_map(
        shards,
        mesh=mesh,
        in_specs=(split, split, turned, turned, split, split, split),
        out_specs=(split, split, split, split),
        check_vma=False,
    )
```

```python
import math

import jax
import jax.numpy as jnp
from jax import lax
from jax.sharding import PartitionSpec as P


def outer_sum(left_rows, right_rows):
    return lax.dot_general(
        left_rows, right_rows, (((0,), (0,)), ((), ())), preferred_element_type=jnp.float32
    )


def inner_last(left_rows, right_rows):
    return lax.dot_general(
        left_rows, right_rows, (((1,), (1,)), ((), ())), preferred_element_type=jnp.float32
    )


def zero_of(*arrays):
    return sum(0.0 * rows[:1, :1].astype(jnp.float32) for rows in arrays)


def line_step(from_left, from_right, step, n):
    return (
        lax.ppermute(from_left, "col", [(i, i + 1) for i in range(step - 1, n - 1)]),
        lax.ppermute(from_right, "col", [(i, i - 1) for i in range(1, n - step + 1)]),
    )


def line_steps(own, n):
    pairs = [(own, own)]
    for step in range(1, n):
        pairs.append(line_step(*pairs[-1], step, n))
    return pairs


def sent_blocks(whole, n, me):
    rows = whole.shape[0] // n

    def block(target):
        return lax.dynamic_slice_in_dim(whole, target * rows, rows, axis=0)

    others = [
        lax.ppermute(
            block(lax.rem(me + k, n)).astype(jnp.bfloat16),
            "col",
            [(i, (i + k) % n) for i in range(n)],
        )
        for k in range(1, n)
    ]
    return block(me), others


def in_turn(pairs, n, me):
    return jnp.concatenate(
        [pairs[0][0]]
        + [jnp.where(me + k < n, pairs[k][1], pairs[n - k][0]) for k in range(1, n)],
        axis=0,
    )


def cuts(width, parts):
    unit = 256 if width % 256 == 0 else 128 if width % 128 == 0 else 1
    units = width // unit
    parts = min(parts, units)
    edges = [unit * -(-units * p // parts) for p in range(parts + 1)]
    return list(zip(edges[:-1], edges[1:]))


def shards(inputs, grad_output, gate_pre, up_pre, gate_weight, up_weight, down_weight):
    n = lax.axis_size("col")
    me = lax.axis_index("col")
    output_cols = lax.all_gather(grad_output, "row", axis=0, tiled=True)
    tokens = output_cols.shape[0]
    block_rows = tokens // n

    gate_value = gate_pre.astype(jnp.float32)
    up_value = up_pre.astype(jnp.float32)
    sigmoid_gate = jax.nn.sigmoid(gate_value)
    hidden = (gate_value * sigmoid_gate * up_value).astype(jnp.bfloat16)
    hidden_pairs = [(hidden, hidden), line_step(hidden, hidden, 1, n)]

    chunks = cuts(gate_pre.shape[1], 2)
    sums = [
        sent_blocks(
            inner_last(output_cols, down_weight[lo:hi]) + zero_of(*hidden_pairs[-1]), n, me
        )
        for lo, hi in chunks
    ]
    input_cols = lax.all_gather(inputs, "row", axis=0, tiled=True)

    pieces = []
    partial_input = None
    pairs = None
    for (lo, hi), (own, others) in zip(chunks, sums):
        grad_hidden = own
        for other in others:
            grad_hidden = grad_hidden + other.astype(jnp.float32)
        if pairs is not None:
            grad_hidden = grad_hidden + zero_of(*pairs[max(n - 2, 0)])
        g = gate_pre[:, lo:hi].astype(jnp.float32)
        u = up_pre[:, lo:hi].astype(jnp.float32)
        s = jax.nn.sigmoid(g)
        grad_gate_pre = (grad_hidden * u * s * (1.0 + g * (1.0 - s))).astype(jnp.bfloat16)
        grad_up_pre = (grad_hidden * (g * s)).astype(jnp.bfloat16)
        both = jnp.concatenate([grad_gate_pre, grad_up_pre], axis=1)
        pairs = line_steps(both, n)
        piece = in_turn(pairs, n, me)
        gate_piece, up_piece = piece[:, : hi - lo], piece[:, hi - lo :]
        part = jnp.dot(
            gate_piece, gate_weight[lo:hi], preferred_element_type=jnp.float32
        ) + jnp.dot(up_piece, up_weight[lo:hi], preferred_element_type=jnp.float32)
        partial_input = part if partial_input is None else partial_input + part
        pieces.append((gate_piece, up_piece))

    after = zero_of(*pairs[-1]).astype(jnp.bfloat16)
    for step in range(2, n):
        tied = [side + after for side in hidden_pairs[-1]]
        hidden_pairs.append(line_step(*tied, step, n))
        after = zero_of(*hidden_pairs[-1]).astype(jnp.bfloat16)
    hidden_rows = in_turn(hidden_pairs, n, me)

    shift = me * block_rows
    partial_input = lax.dynamic_slice_in_dim(
        jnp.concatenate([partial_input, partial_input], axis=0), tokens - shift, tokens, axis=0
    )
    grad_input = lax.psum_scatter(partial_input, "row", scatter_dimension=0, tiled=True)

    def turned(rows):
        return lax.dynamic_slice_in_dim(
            jnp.concatenate([rows, rows], axis=0), shift, tokens, axis=0
        )

    input_rows, output_rows = turned(input_cols), turned(output_cols)
    gate_rows = jnp.concatenate([p[0] for p in pieces], axis=1)
    up_rows = jnp.concatenate([p[1] for p in pieces], axis=1)
    factor = 1.0 / math.sqrt(tokens)
    return (
        grad_input,
        outer_sum(gate_rows, input_rows) * factor,
        outer_sum(up_rows, input_rows) * factor,
        outer_sum(hidden_rows, output_rows) * factor,
    )


def solution(mesh):
    split, turned = P("row", "col"), P("col", "row")
    return jax.shard_map(
        shards,
        mesh=mesh,
        in_specs=(split, split, turned, turned, split, split, split),
        out_specs=(split, split, split, split),
        check_vma=False,
    )
```
